32 devices in a mesh: ctx: 8 (over z, x), tp: 4 (over y, core).
Axes of the slice: x: 2, y: 2, z: 4, core: 2. Of those that a mesh axis runs over, the one named last changes fastest.
Arguments:
- hidden_in: bfloat16 [2, 1024, 1024], P(None, 'ctx'), may hold values from -6 to 6
- seg_ids: int32 [2, 1024], replicated, may hold values from 0 to 4, as said below
- first_gain: float32 [1024], replicated, may hold values from 0.5 to 1.5
- query_weight: bfloat16 [1024, 1024], P(None, 'tp'), may hold values from -0.1875 to 0.1875
- keyval_weight: bfloat16 [1024, 512], replicated, may hold values from -0.1875 to 0.1875
- attn_out_weight: bfloat16 [1024, 1024], P('tp'), may hold values from -0.75 to 0.75
- mixin_weight: bfloat16 [1024, 1536], P(None, 'tp'), may hold values from -0.1875 to 0.1875
- mixgate_weight: bfloat16 [1024, 1536], P(None, 'tp'), may hold values from -0.1875 to 0.1875
- inject_weight: bfloat16 [1024, 128], replicated, may hold values from -0.00390625 to 0.00390625
- readout_weight: bfloat16 [1024, 128], replicated, may hold values from -0.1875 to 0.1875
- step_weight: bfloat16 [1024, 24], P(None, 'tp'), may hold values from -0.1875 to 0.1875
- step_bias: float32 [24], P('tp'), may hold values from -1 to 1
- decay_rate: float32 [24], P('tp'), may hold values from 0.00029296876 to 0.06
- skip_gain: float32 [24], P('tp'), may hold values from 0.5 to 1.5
- mixout_weight: bfloat16 [1536, 1024], P('tp'), may hold values from -0.15625 to 0.15625
- second_gain: float32 [1024], replicated, may hold values from 0.5 to 1.5
- gate_weight: bfloat16 [1024, 2048], P(None, 'tp'), may hold values from -0.1875 to 0.1875
- up_weight: bfloat16 [1024, 2048], P(None, 'tp'), may hold values from -0.1875 to 0.1875
- down_weight: bfloat16 [2048, 1024], P('tp'), may hold values from -0.125 to 0.125
- cotangent: bfloat16 [2, 1024, 1024], P(None, 'ctx'), may hold values from -6 to 6
Outputs:
- layer_out: bfloat16 [2, 1024, 1024], P(None, 'ctx')
- grad_hidden: float32 [2, 1024, 1024], P(None, 'ctx')
- grad_first_gain: float32 [1024], replicated
- grad_query: float32 [1024, 1024], P('ctx', 'tp')
- grad_keyval: float32 [1024, 512], P(('ctx', 'tp'))
- grad_attn_out: float32 [1024, 1024], P('tp', 'ctx')
- grad_mixin: float32 [1024, 1536], P('ctx', 'tp')
- grad_mixgate: float32 [1024, 1536], P('ctx', 'tp')
- grad_inject: float32 [1024, 128], P(('ctx', 'tp'))
- grad_readout: float32 [1024, 128], P(('ctx', 'tp'))
- grad_step: float32 [1024, 24], P('ctx', 'tp')
- grad_step_bias: float32 [24], P('tp')
- grad_decay_rate: float32 [24], P('tp')
- grad_skip_gain: float32 [24], P('tp')
- grad_mixout: float32 [1536, 1024], P('tp', 'ctx')
- grad_second_gain: float32 [1024], replicated
- grad_gate: float32 [1024, 2048], P('ctx', 'tp')
- grad_up: float32 [1024, 2048], P('ctx', 'tp')
- grad_down: float32 [2048, 1024], P('tp', 'ctx')
The draws below stay inside these ranges and needn't reach their ends.
Inputs may be any that keep to these rules, and one draw needn't show every extreme that they name: `seg_ids`: within each sequence the ids never fall and start at 0; in one sequence of each draw all ids are 0, in every other one the last position has id 4.
All inputs are finite; a program needn't handle non-finite values.
Results may differ from the reference program's by a relative error of at most 0.025.
Values may be sent and summed in bfloat16 or wider, within the bound.
A program may use at most 128 MiB of HBM per device.

```python
import math
import jax
import jax.numpy as jnp
from jax import lax

D = 1024
QHEADS = 8
KVHEADS = 2
HEAD = 128
HEADS = 24
HEAD_M = 64
N_STATE = 128
FF = 2048
BLK = 64
SEQS = 2
LENGTH = 1024
N_CTX = 8


def draw_seg_ids(key, part):
    key = jax.random.fold_in(key, 7)
    cut_key, pick_key = jax.random.split(key)
    cuts = jax.random.randint(cut_key, (SEQS, 4), 1, LENGTH)
    single = jax.random.randint(pick_key, (), 0, SEQS)
    places = jnp.arange(LENGTH)
    numbers = jnp.sum((places[None, :, None] >= cuts[:, None, :]).astype(jnp.int32), axis=-1)
    return jnp.where(jnp.arange(SEQS)[:, None] == single, 0, numbers).astype(jnp.int32)


def shard_levels(rng, shape, cuts, smallest, high):
    def one(dim, blocks):
        draws = jax.random.uniform(jax.random.fold_in(jax.random.fold_in(rng, 6), dim), (blocks,), jnp.float32, smallest / len(cuts), high / len(cuts))
        return jnp.repeat(jnp.exp(draws), shape[dim] // blocks).reshape((-1,) + (1,) * (len(shape) - dim - 1))

    loudness = one(*cuts[0])
    for cut in cuts[1:]:
        loudness = loudness * one(*cut)
    return loudness


def centred(stream_key, dims, spread, reach, cuts=(), kind=jnp.bfloat16):
    values = spread * jax.random.normal(stream_key, dims, jnp.float32)
    if cuts:
        values = values * shard_levels(stream_key, dims, cuts, -0.22, 0.18)
    return jnp.clip(values, -reach, reach).astype(kind)


def setup_inputs(seed: int = 0) -> dict:
    key_list = jax.random.split(jax.random.key(seed), 21)
    hidden_in = centred(key_list[0], (SEQS, LENGTH, D), 1.0, 6.0, ((1, 8),))
    seg_ids = draw_seg_ids(jax.random.fold_in(key_list[20], 71), 0)
    first_gain = jnp.clip(1.0 + 0.1 * jax.random.normal(key_list[2], (D,), jnp.float32), 0.5, 1.5)
    query_weight = centred(key_list[3], (D, QHEADS * HEAD), D ** -0.5, 0.1875, ((1, 4),))
    keyval_weight = centred(key_list[4], (D, 2 * KVHEADS * HEAD), D ** -0.5, 0.1875)
    attn_out_weight = centred(key_list[5], (QHEADS * HEAD, D), (QHEADS * HEAD // 16) ** -0.5, 0.75, ((0, 4),))
    mixin_weight = centred(key_list[6], (D, HEADS * HEAD_M), D ** -0.5, 0.1875, ((1, 4),))
    mixgate_weight = centred(key_list[7], (D, HEADS * HEAD_M), D ** -0.5, 0.1875, ((1, 4),))
    inject_weight = centred(key_list[8], (D, N_STATE), (D * N_STATE * LENGTH // 64) ** -0.5, 0.00390625)
    readout_weight = centred(key_list[9], (D, N_STATE), D ** -0.5, 0.1875)
    step_weight = centred(key_list[10], (D, HEADS), D ** -0.5, 0.1875, ((1, 4),))
    step_bias = jnp.clip(jax.random.uniform(key_list[11], (HEADS,), jnp.float32, -1.0, 1.0) * shard_levels(key_list[11], (HEADS,), ((0, 4),), -0.4, 0.0), -1.0, 1.0)
    decay_rate = jnp.clip(jnp.exp(math.log(0.06) - 5.322034 * jax.random.uniform(key_list[12], (HEADS,), jnp.float32) ** shard_levels(key_list[12], (HEADS,), ((0, 4),), -0.2, 0.2)), 0.00029296876, 0.06)
    skip_gain = jnp.clip(0.5 + 1.0 * jax.random.uniform(key_list[13], (HEADS,), jnp.float32) ** shard_levels(key_list[13], (HEADS,), ((0, 4),), -0.2, 0.2), 0.5, 1.5)
    mixout_weight = centred(key_list[14], (HEADS * HEAD_M, D), (HEADS * HEAD_M) ** -0.5, 0.15625, ((0, 4),))
    second_gain = jnp.clip(1.0 + 0.1 * jax.random.normal(key_list[15], (D,), jnp.float32), 0.5, 1.5)
    gate_weight = centred(key_list[16], (D, FF), D ** -0.5, 0.1875, ((1, 4),))
    up_weight = centred(key_list[17], (D, FF), D ** -0.5, 0.1875, ((1, 4),))
    down_weight = centred(key_list[18], (FF, D), FF ** -0.5, 0.125, ((0, 4),))
    cotangent = centred(key_list[19], (SEQS, LENGTH, D), 1.0, 6.0, ((1, 8),))
    return dict(hidden_in=hidden_in, seg_ids=seg_ids, first_gain=first_gain, query_weight=query_weight, keyval_weight=keyval_weight, attn_out_weight=attn_out_weight, mixin_weight=mixin_weight, mixgate_weight=mixgate_weight, inject_weight=inject_weight, readout_weight=readout_weight, step_weight=step_weight, step_bias=step_bias, decay_rate=decay_rate, skip_gain=skip_gain, mixout_weight=mixout_weight, second_gain=second_gain, gate_weight=gate_weight, up_weight=up_weight, down_weight=down_weight, cotangent=cotangent)


@jax.custom_vjp
def low(v):
    return lax.optimization_barrier(v.astype(jnp.bfloat16)).astype(jnp.float32)

@jax.custom_vjp
def low_back(v):
    return v

def low_keep(v):
    return (low(v), None)

def low_pass(kept, grad):
    return (grad,)

def back_keep(v):
    return (v, None)

def back_low(kept, grad):
    return (low(grad),)
low.defvjp(low_keep, low_pass)
low_back.defvjp(back_keep, back_low)
NORM_EPS = 1e-05
MASK_FILL = -1e+30
FAR_BELOW = -10000.0
exact_precision = lax.Precision.HIGHEST

def decays(step_raw, decay_rate):
    step_size = jax.nn.softplus(step_raw)
    return (step_size, jnp.cumsum(-decay_rate[None, :] * step_size, axis=0))

def state_part(mix_in, key_vec, step_size, log_decay, seg_here, seg_before):
    log_end = log_decay[-1]
    same_end = (seg_here == seg_here[-1]).astype(jnp.float32)
    end_weight = jnp.exp(log_end[None, :] - log_decay) * same_end[:, None] * step_size
    state = jnp.einsum('sh,shp,sn->hpn', end_weight, mix_in, key_vec, precision=exact_precision)
    carried = jnp.exp(log_end) * (seg_here[-1] == seg_before).astype(jnp.float32)
    return (carried, state)

def out_part(mix_in, key_vec, read_vec, step_size, log_decay, skip_gain, seg_here, seg_before, state_in):
    places = jnp.arange(seg_here.shape[0], dtype=jnp.int32)
    visible = (places[:, None] >= places[None, :]) & (seg_here[:, None] == seg_here[None, :])
    log_gap = log_decay[:, None, :] - log_decay[None, :, :]
    weights = jnp.exp(jnp.where(visible[:, :, None], log_gap, FAR_BELOW)) * step_size[None, :, :]
    mixing = jnp.einsum('tn,sn->ts', read_vec, key_vec, precision=exact_precision)
    result = jnp.einsum('tsh,shp->thp', weights * mixing[:, :, None], mix_in, precision=exact_precision)
    entry = jnp.exp(log_decay) * (seg_here == seg_before).astype(jnp.float32)[:, None]
    result = result + entry[:, :, None] * jnp.einsum('tn,hpn->thp', read_vec, state_in, precision=exact_precision)
    return result + skip_gain[None, :, None] * mix_in

def block_scan(mix_in, key_vec, read_vec, step_raw, decay_rate, skip_gain, seg_here, seg_before, state_in):
    step_size, log_decay = decays(step_raw, decay_rate)
    carried, state = state_part(mix_in, key_vec, step_size, log_decay, seg_here, seg_before)
    result = out_part(mix_in, key_vec, read_vec, step_size, log_decay, skip_gain, seg_here, seg_before, state_in)
    return (result, carried, state)

def rms_scale(value_rows):
    return lax.rsqrt(lax.optimization_barrier(jnp.mean(value_rows * value_rows, axis=-1, keepdims=True)) + NORM_EPS)

def project(value_rows, weight_matrix):
    return jnp.einsum('zbt,tm->zbm', value_rows, weight_matrix, precision=exact_precision)

def natural(value_rows):
    shape = value_rows.shape
    split = value_rows.reshape((shape[0], N_CTX, 2, BLK) + shape[2:])
    ordered = jnp.concatenate([split[:, :, 0], jnp.flip(split[:, :, 1], axis=1)], axis=1)
    return ordered.reshape(shape)

def dealt(value_rows):
    shape = value_rows.shape
    split = value_rows.reshape((shape[0], 2 * N_CTX, BLK) + shape[2:])
    paired = jnp.stack([split[:, :N_CTX], jnp.flip(split[:, N_CTX:], axis=1)], axis=2)
    return paired.reshape(shape)

def attention_seq(queries, keys, value_rows, seg_row):
    group = QHEADS // KVHEADS
    keys_all = jnp.repeat(keys, group, axis=1)
    values_all = jnp.repeat(value_rows, group, axis=1)
    q_block = math.gcd(LENGTH, 512)
    places = jnp.arange(LENGTH, dtype=jnp.int32)
    starts = jnp.arange(LENGTH // q_block, dtype=jnp.int32) * q_block
    blocks_q = queries.reshape(LENGTH // q_block, q_block, QHEADS, HEAD)

    def one_block(pieces):
        query_rows, start = pieces
        q_places = start + jnp.arange(q_block, dtype=jnp.int32)
        q_segs = lax.dynamic_slice_in_dim(seg_row, start, q_block, 0)
        scores = low_back(jnp.einsum('qhd,khd->qhk', query_rows, keys_all, precision=exact_precision) * HEAD ** (-0.5))
        visible = (places[None, :] <= q_places[:, None]) & (seg_row[None, :] == q_segs[:, None])
        scores = jnp.where(visible[:, None, :], scores, MASK_FILL)
        probs = jax.nn.softmax(scores, axis=-1)
        return jnp.einsum('qhk,khd->qhd', low(probs), values_all, precision=exact_precision)
    attended = lax.map(jax.checkpoint(one_block), (blocks_q, starts))
    return attended.reshape(LENGTH, QHEADS, HEAD)

def mamba_seq(mix_in, key_vec, read_vec, step_raw, seg_row, decay_rate, skip_gain):
    block_count = LENGTH // BLK
    seg_blocks = seg_row.reshape(block_count, BLK)
    seg_before = jnp.concatenate([jnp.full((1,), -1, jnp.int32), seg_blocks[:-1, -1]])

    def advance(state_in, pieces):
        mix_b, key_b, read_b, step_b, seg_b, before_b = pieces
        result, carried, state = block_scan(mix_b, key_b, read_b, step_b, decay_rate, skip_gain, seg_b, before_b, state_in)
        return (carried[:, None, None] * state_in + state, result)
    start_state = jnp.zeros((HEADS, HEAD_M, N_STATE), jnp.float32)
    pieces = (mix_in.reshape(block_count, BLK, HEADS, HEAD_M), key_vec.reshape(block_count, BLK, N_STATE), read_vec.reshape(block_count, BLK, N_STATE), step_raw.reshape(block_count, BLK, HEADS), seg_blocks, seg_before)
    _, results = lax.scan(jax.checkpoint(advance), start_state, pieces)
    return results.reshape(LENGTH, HEADS, HEAD_M)

def layer(hidden, seg_ids, first_gain, query_weight, keyval_weight, attn_out_weight, mixin_weight, mixgate_weight, inject_weight, readout_weight, step_weight, step_bias, decay_rate, skip_gain, mixout_weight, second_gain, gate_weight, up_weight, down_weight):
    seq_count = hidden.shape[0]
    normed = low(hidden * rms_scale(hidden) * first_gain)
    queries = low(low_back(project(normed, query_weight))).reshape(seq_count, LENGTH, QHEADS, HEAD)
    keyval = low(low_back(project(normed, keyval_weight))).reshape(seq_count, LENGTH, KVHEADS, 2, HEAD)
    attended = jax.vmap(attention_seq)(queries, keyval[:, :, :, 0], keyval[:, :, :, 1], seg_ids)
    attended = low(low_back(attended.reshape(seq_count, LENGTH, QHEADS * HEAD)))
    mix_in = low(low_back(project(normed, mixin_weight))).reshape(seq_count, LENGTH, HEADS, HEAD_M)
    mix_gate = low_back(project(normed, mixgate_weight))
    key_vec = low(low_back(project(normed, inject_weight)))
    read_vec = low(low_back(project(normed, readout_weight)))
    step_raw = low_back(project(normed, step_weight)) + step_bias
    mixed = jax.vmap(mamba_seq, in_axes=(0, 0, 0, 0, 0, None, None))(mix_in, key_vec, read_vec, step_raw, seg_ids, decay_rate, skip_gain)
    gated = low(low_back(mixed.reshape(seq_count, LENGTH, HEADS * HEAD_M) * jax.nn.silu(mix_gate)))
    branch = low_back(project(attended, attn_out_weight) + project(gated, mixout_weight))
    middle = hidden + branch
    normed_two = low(middle * rms_scale(middle) * second_gain)
    gate = low_back(project(normed_two, gate_weight))
    up_val = low_back(project(normed_two, up_weight))
    inner = low(jax.nn.silu(gate) * up_val)
    return middle + project(inner, down_weight)

def reference(hidden_in, seg_ids, first_gain, query_weight, keyval_weight, attn_out_weight, mixin_weight, mixgate_weight, inject_weight, readout_weight, step_weight, step_bias, decay_rate, skip_gain, mixout_weight, second_gain, gate_weight, up_weight, down_weight, cotangent):
    params = tuple((value.astype(jnp.float32) for value in (first_gain, query_weight, keyval_weight, attn_out_weight, mixin_weight, mixgate_weight, inject_weight, readout_weight, step_weight, step_bias, decay_rate, skip_gain, mixout_weight, second_gain, gate_weight, up_weight, down_weight)))
    hidden = natural(hidden_in.astype(jnp.float32))
    cot_nat = natural(cotangent.astype(jnp.float32))

    def forward(value_rows, *weights):
        return layer(value_rows, seg_ids, *weights)
    result, backward_function = jax.vjp(forward, hidden, *params)
    grads = backward_function(cot_nat)
    return (dealt(result).astype(jnp.bfloat16), dealt(grads[0]), grads[1], grads[2], grads[3], grads[4], grads[5], grads[6], grads[7], grads[8], grads[9], grads[10], grads[11], grads[12], grads[13], grads[14], grads[15], grads[16], grads[17])
```

```python
import jax
import jax.numpy as jnp
from jax import lax
from jax.sharding import PartitionSpec as P

QHEADS = 8
KVHEADS = 2
HEAD = 128


NORM_EPS = 1e-05
MASK_FILL = -1e30
FAR_BELOW = -10000.0
exact_precision = lax.Precision.HIGHEST


def spread(array, axes):
    return lax.all_to_all(array, axes, 0, 0, tiled=True)


def row_chunks(array, count):
    return array.reshape((count, array.shape[0] // count) + array.shape[1:])


def three_parts(value):
    high = lax.reduce_precision(value, 8, 7)
    rest = value - high
    mid = lax.reduce_precision(rest, 8, 7)
    return jnp.stack([high, mid, rest - mid]).astype(jnp.bfloat16)


def decays(step_raw, decay_rate):
    step_size = jax.nn.softplus(step_raw)
    return (step_size, jnp.cumsum(-decay_rate[None, :] * step_size, axis=0))


def state_part(mix_in, key_vec, step_size, log_decay, seg_here, seg_before):
    log_end = log_decay[-1]
    same_end = (seg_here == seg_here[-1]).astype(jnp.float32)
    end_weight = jnp.exp(log_end[None, :] - log_decay) * same_end[:, None] * step_size
    state = jnp.einsum("sh,shp,sn->hpn", end_weight, mix_in, key_vec, precision=exact_precision)
    carried = jnp.exp(log_end) * (seg_here[-1] == seg_before).astype(jnp.float32)
    return (carried, state)


def out_part(
    mix_in, key_vec, read_vec, step_size, log_decay, skip_gain, seg_here, seg_before, state_in
):
    places = jnp.arange(seg_here.shape[0], dtype=jnp.int32)
    visible = (places[:, None] >= places[None, :]) & (seg_here[:, None] == seg_here[None, :])
    log_gap = log_decay[:, None, :] - log_decay[None, :, :]
    weights = jnp.exp(jnp.where(visible[:, :, None], log_gap, FAR_BELOW)) * step_size[None, :, :]
    mixing = jnp.einsum("tn,sn->ts", read_vec, key_vec, precision=exact_precision)
    result = jnp.einsum(
        "tsh,shp->thp", weights * mixing[:, :, None], mix_in, precision=exact_precision
    )
    entry = jnp.exp(log_decay) * (seg_here == seg_before).astype(jnp.float32)[:, None]
    result = result + entry[:, :, None] * jnp.einsum(
        "tn,hpn->thp", read_vec, state_in, precision=exact_precision
    )
    return result + skip_gain[None, :, None] * mix_in


def block_scan(
    mix_in, key_vec, read_vec, step_raw, decay_rate, skip_gain, seg_here, seg_before, state_in
):
    step_size, log_decay = decays(step_raw, decay_rate)
    carried, state = state_part(mix_in, key_vec, step_size, log_decay, seg_here, seg_before)
    result = out_part(
        mix_in, key_vec, read_vec, step_size, log_decay, skip_gain, seg_here, seg_before, state_in
    )
    return (result, carried, state)


def over_blocks(function, axes):
    return jax.vmap(jax.vmap(function, in_axes=axes), in_axes=axes)


def rms_scale(value_rows):
    return lax.rsqrt(jnp.mean(value_rows * value_rows, axis=-1, keepdims=True) + NORM_EPS)


def norm_back(d_norm, gain, value_rows, scale):
    d_hat = d_norm * gain
    return scale * d_hat - value_rows * scale**3 * jnp.mean(
        d_hat * value_rows, axis=-1, keepdims=True
    )


def times_trans(grad, weight_matrix):
    return lax.dot_general(
        grad,
        weight_matrix,
        (((grad.ndim - 1,), (1,)), ((), ())),
        preferred_element_type=jnp.float32,
    )


def outer_rows(left, right):
    return lax.dot_general(
        left, right, (((0,), (0,)), ((), ())), preferred_element_type=jnp.float32
    )


def body(
    hidden_in,
    seg_ids,
    first_gain,
    query_weight,
    keyval_weight,
    attn_out_weight,
    mixin_weight,
    mixgate_weight,
    inject_weight,
    readout_weight,
    step_weight,
    step_bias,
    decay_rate,
    skip_gain,
    mixout_weight,
    second_gain,
    gate_weight,
    up_weight,
    down_weight,
    cotangent,
):
    ctx_size = lax.axis_size("ctx")
    tp_size = lax.axis_size("tp")
    ctx_index = lax.axis_index("ctx")
    tp_index = lax.axis_index("tp")
    seq_count, row_count, width = hidden_in.shape
    block_rows = row_count // 2
    block_count = 2 * ctx_size
    q_local = query_weight.shape[1] // HEAD
    heads_local = step_weight.shape[1]
    inner_local = mixin_weight.shape[1]
    mamba_head = inner_local // heads_local
    n_state = inject_weight.shape[1]
    ff_local = gate_weight.shape[1]
    kv_head = tp_index * q_local // (QHEADS // KVHEADS)
    scale = HEAD ** (-0.5)
    all_rows = seq_count * row_count

    local_rows = jnp.arange(row_count, dtype=jnp.int32)
    devices = jnp.arange(ctx_size, dtype=jnp.int32)

    def positions(device, local):
        return jnp.where(
            local < block_rows,
            device * block_rows + local,
            (block_count - 1 - device) * block_rows + local - block_rows,
        )

    q_places = positions(ctx_index, local_rows)
    k_places = positions(devices[:, None], local_rows[None, :]).reshape(-1)
    seg_by_block = seg_ids.reshape(seq_count, block_count, block_rows)
    k_segs = jnp.concatenate(
        [seg_by_block[:, :ctx_size], seg_by_block[:, ctx_size:][:, ::-1]], axis=2
    ).reshape(seq_count, ctx_size * row_count)
    q_segs = lax.dynamic_slice_in_dim(k_segs, ctx_index * row_count, row_count, 1)
    seg_end = seg_by_block[:, :, -1]
    own_blocks = jnp.stack([ctx_index, block_count - 1 - ctx_index])
    block_ids = jnp.arange(block_count, dtype=jnp.int32)
    is_before = block_ids[None, :] == own_blocks[:, None] - 1
    seg_before = jnp.sum(
        jnp.where(is_before[None], seg_end[:, None, :], 0), axis=-1
    ) - jnp.where(own_blocks == 0, 1, 0)

    step_pad = -heads_local % 128
    step_cols = heads_local + step_pad
    keyval_mine = lax.dynamic_slice_in_dim(keyval_weight, kv_head * 2 * HEAD, 2 * HEAD, 1)
    step_wide = jnp.pad(step_weight, ((0, 0), (0, step_pad)))
    weights_in = jnp.concatenate(
        [
            query_weight,
            mixin_weight,
            step_wide,
            mixgate_weight,
            keyval_mine,
            inject_weight,
            readout_weight,
        ],
        axis=1,
    )
    sizes_in = (
        q_local * HEAD,
        inner_local,
        step_cols,
        inner_local,
        2 * HEAD,
        n_state,
        n_state,
    )
    bounds = []
    at = 0
    for size in sizes_in:
        at += size
        bounds.append(at)

    hidden = hidden_in.astype(jnp.float32).reshape(all_rows, width)
    cotan = cotangent.reshape(all_rows, width)
    first_scale = rms_scale(hidden)
    normed = (hidden * first_scale * first_gain).astype(jnp.bfloat16)
    projected = jnp.dot(normed, weights_in, preferred_element_type=jnp.float32)
    queries, mix_in, step_raw, mix_gate, keyval, key_vec, read_vec = jnp.split(
        projected, bounds[:-1], axis=1
    )
    queries = queries.astype(jnp.bfloat16).reshape(seq_count, row_count, q_local, HEAD)
    keyval = keyval.astype(jnp.bfloat16).reshape(seq_count, row_count, 2 * HEAD)
    mix_in = mix_in.astype(jnp.bfloat16)
    key_vec = key_vec.astype(jnp.bfloat16)
    read_vec = read_vec.astype(jnp.bfloat16)
    step_raw = step_raw[:, :heads_local] + step_bias

    def blocked(value_rows, tail):
        return value_rows.reshape((seq_count, 2, block_rows) + tail)

    mix_blocks = blocked(mix_in.astype(jnp.float32), (heads_local, mamba_head))
    key_blocks = blocked(key_vec.astype(jnp.float32), (n_state,))
    read_blocks = blocked(read_vec.astype(jnp.float32), (n_state,))
    step_blocks = blocked(step_raw, (heads_local,))
    seg_blocks = blocked(q_segs, ())
    step_size, log_decay = over_blocks(decays, (0, None))(step_blocks, decay_rate)

    log_end = log_decay[:, :, -1, :].reshape(seq_count, 2 * heads_local)
    parts = jnp.moveaxis(three_parts(log_end), 0, 1).reshape(seq_count, 1, 6 * heads_local)
    extra_rows = jnp.pad(parts, ((0, 0), (0, 15), (0, 2 * HEAD - 6 * heads_local)))
    gathered = lax.all_gather(jnp.concatenate([keyval, extra_rows], axis=1), "ctx")
    keyval_all = jnp.swapaxes(gathered[:, :, :row_count], 0, 1).reshape(
        seq_count, ctx_size * row_count, 2 * HEAD
    )
    keys_all, values_all = keyval_all[..., :HEAD], keyval_all[..., HEAD:]
    decay_all = jnp.sum(
        gathered[:, :, row_count, : 6 * heads_local]
        .astype(jnp.float32)
        .reshape(ctx_size, seq_count, 3, 2, heads_local),
        axis=2,
    )
    log_blocks = jnp.concatenate([decay_all[:, :, 0], decay_all[::-1, :, 1]], axis=0)
    log_sum = jnp.cumsum(log_blocks, axis=0)

    log_prev = jnp.concatenate([jnp.zeros_like(log_sum[:1]), log_sum[:-1]], axis=0)
    seg_end_t = seg_end.T
    seg_prev_t = jnp.concatenate([jnp.full_like(seg_end_t[:1], -1), seg_end_t[:-1]], axis=0)

    def picked(table):
        return jnp.stack(
            [
                lax.dynamic_index_in_dim(table, own_blocks[0], 0, keepdims=False),
                lax.dynamic_index_in_dim(table, own_blocks[1], 0, keepdims=False),
            ]
        )

    def block_weights(valid, gap):
        weight = jnp.exp(jnp.where(valid[..., None], gap, FAR_BELOW))
        weight = jnp.where(valid[..., None], weight, 0.0)
        halves = jnp.stack([weight[:, :ctx_size], weight[:, ctx_size:][:, ::-1]], axis=2)
        return halves

    order = block_ids[None, :, None]
    own = own_blocks[:, None, None]
    rise = block_weights(
        (order < own) & (seg_end_t[None] == picked(seg_prev_t)[:, None]),
        picked(log_prev)[:, None] - log_sum[None],
    )
    fall = block_weights(
        (order > own) & (seg_prev_t[None] == picked(seg_end_t)[:, None]),
        log_prev[None] - picked(log_sum)[:, None],
    )

    def weighted(weight, blocks):
        total = 0.0
        for half in range(2):
            total = total + jnp.sum(
                weight[:, :, half][..., None, None]
                * blocks[None, :, :, half].astype(jnp.float32),
                axis=1,
            )
        return jnp.swapaxes(total, 0, 1)

    carried, state = over_blocks(state_part, (0, 0, 0, 0, 0, 0))(
        mix_blocks, key_blocks, step_size, log_decay, seg_blocks, seg_before
    )
    state_all = lax.all_gather(state.astype(jnp.bfloat16), "ctx")

    scores = (
        jnp.einsum("srhd,skd->srhk", queries, keys_all, preferred_element_type=jnp.float32) * scale
    )
    visible = (k_places[None, None, :] <= q_places[None, :, None]) & (
        k_segs[:, None, :] == q_segs[:, :, None]
    )
    scores = jnp.where(visible[:, :, None, :], scores, MASK_FILL)
    top = jnp.max(scores, axis=-1, keepdims=True)
    raised = jnp.exp(scores - top)
    probs = raised / jnp.sum(raised, axis=-1, keepdims=True)
    probs_low = probs.astype(jnp.bfloat16)
    attn_full = jnp.einsum(
        "srhk,skd->srhd", probs_low, values_all, preferred_element_type=jnp.float32
    )
    attn_low = attn_full.astype(jnp.bfloat16).reshape(all_rows, q_local * HEAD)

    state_in = weighted(rise, state_all)
    mixed = over_blocks(out_part, (0, 0, 0, 0, 0, None, 0, 0, 0))(
        mix_blocks,
        key_blocks,
        read_blocks,
        step_size,
        log_decay,
        skip_gain,
        seg_blocks,
        seg_before,
        state_in,
    )
    mixed = mixed.reshape(all_rows, inner_local)
    mixgate_sig = jax.nn.sigmoid(mix_gate)
    gate_act = mix_gate * mixgate_sig
    gated = (mixed * gate_act).astype(jnp.bfloat16)
    branch_in = jnp.concatenate([attn_low, gated], axis=1)
    weights_out = jnp.concatenate([attn_out_weight, mixout_weight], axis=0)
    branch = lax.psum(
        jnp.dot(branch_in, weights_out, preferred_element_type=jnp.float32).astype(jnp.bfloat16),
        "tp",
    ).astype(jnp.float32)
    middle = hidden + branch
    second_scale = rms_scale(middle)
    normed_two = (middle * second_scale * second_gain).astype(jnp.bfloat16)
    weights_ff = jnp.concatenate([gate_weight, up_weight], axis=1)
    gate_up = jnp.dot(normed_two, weights_ff, preferred_element_type=jnp.float32)
    gate, up_val = gate_up[:, :ff_local], gate_up[:, ff_local:]
    gate_sig = jax.nn.sigmoid(gate)
    inner = (gate * gate_sig * up_val).astype(jnp.bfloat16)
    inner_gradient = times_trans(cotan, down_weight)
    d_gate = (inner_gradient * up_val * gate_sig * (1.0 + gate * (1.0 - gate_sig))).astype(
        jnp.bfloat16
    )
    d_up = (inner_gradient * gate * gate_sig).astype(jnp.bfloat16)
    d_gate_up = jnp.concatenate([d_gate, d_up], axis=1)
    second_normed_gradient = lax.psum(
        times_trans(d_gate_up, weights_ff).astype(jnp.bfloat16), "tp"
    ).astype(jnp.float32)
    mlp_out = lax.psum(
        jnp.dot(inner, down_weight, preferred_element_type=jnp.float32).astype(jnp.bfloat16), "tp"
    )

    def outer_low(left, right):
        return outer_rows(left, right).astype(jnp.bfloat16)

    ff_grads = spread(
        row_chunks(
            jnp.concatenate([outer_low(normed_two, d_gate_up), outer_low(cotan, inner)], axis=1),
            ctx_size,
        ),
        "ctx",
    )

    grad_second = jnp.sum(second_normed_gradient * middle * second_scale, axis=0)
    d_middle = cotan.astype(jnp.float32) + norm_back(
        second_normed_gradient, second_gain, middle, second_scale
    )
    d_branch = d_middle.astype(jnp.bfloat16)
    d_branch_in = times_trans(d_branch, weights_out).astype(jnp.bfloat16)
    d_attn = d_branch_in[:, : q_local * HEAD].reshape(seq_count, row_count, q_local, HEAD)
    d_gated = d_branch_in[:, q_local * HEAD :].astype(jnp.float32)
    d_mixed = d_gated * gate_act
    d_mix_gate = (d_gated * mixed * mixgate_sig * (1.0 + mix_gate * (1.0 - mixgate_sig))).astype(
        jnp.bfloat16
    )

    d_mixed_blocks = blocked(d_mixed, (heads_local, mamba_head))
    entry = (
        jnp.exp(log_decay) * (seg_blocks == seg_before[..., None]).astype(jnp.float32)[..., None]
    )
    local_grad = jnp.einsum(
        "abth,abthp,abtn->abhpn", entry, d_mixed_blocks, read_blocks, precision=exact_precision
    )
    grad_all = lax.all_gather(local_grad.astype(jnp.bfloat16), "ctx")

    delta = jnp.sum(d_attn.astype(jnp.float32) * attn_full, axis=-1, keepdims=True)
    d_probs = jnp.einsum("srhd,skd->srhk", d_attn, values_all, preferred_element_type=jnp.float32)
    d_scores = (probs * (d_probs - delta)).astype(jnp.bfloat16)
    d_keys = (
        jnp.einsum("srhk,srhd->skd", d_scores, queries, preferred_element_type=jnp.float32) * scale
    ).astype(jnp.bfloat16)
    d_values = jnp.einsum(
        "srhk,srhd->skd", probs_low, d_attn, preferred_element_type=jnp.float32
    ).astype(jnp.bfloat16)
    d_keyval = jnp.concatenate([d_keys, d_values], axis=-1).reshape(
        seq_count, ctx_size, row_count, 2 * HEAD
    )
    d_keyval = spread(jnp.swapaxes(d_keyval, 0, 1), "ctx")
    d_query = (
        jnp.einsum("srhk,skd->srhd", d_scores, keys_all, preferred_element_type=jnp.float32) * scale
    )
    d_query = d_query.astype(jnp.bfloat16).reshape(all_rows, q_local * HEAD)
    out_grads = spread(
        row_chunks(
            jnp.concatenate([outer_low(d_branch, branch_in), outer_low(normed, d_mix_gate)], axis=1),
            ctx_size,
        ),
        "ctx",
    )
    d_keyval = jnp.sum(d_keyval.astype(jnp.float32), axis=0).astype(jnp.bfloat16)
    d_keyval = d_keyval.reshape(all_rows, 2 * HEAD)

    grad_end = weighted(fall, grad_all)
    decay_cot = jnp.sum(grad_end * state_in, axis=(-2, -1))

    def whole(mix_vals, key_vals, read_vals, step_vals, rate_vals, skip_vals, state_vals):
        return over_blocks(block_scan, (0, 0, 0, 0, None, None, 0, 0, 0))(
            mix_vals,
            key_vals,
            read_vals,
            step_vals,
            rate_vals,
            skip_vals,
            seg_blocks,
            seg_before,
            state_vals,
        )

    _, backward_function = jax.vjp(
        whole, mix_blocks, key_blocks, read_blocks, step_blocks, decay_rate, skip_gain, state_in
    )
    grad_mix, grad_key, grad_read, grad_stepv, grad_rate, grad_skip, _ = backward_function(
        (d_mixed_blocks, decay_cot, grad_end)
    )
    d_mix_in = grad_mix.reshape(all_rows, inner_local).astype(jnp.bfloat16)
    d_key_vec = grad_key.reshape(all_rows, n_state).astype(jnp.bfloat16)
    d_read_vec = grad_read.reshape(all_rows, n_state).astype(jnp.bfloat16)
    d_step_raw = grad_stepv.reshape(all_rows, heads_local)
    grad_bias = jnp.sum(d_step_raw, axis=0)
    d_step_wide = jnp.pad(d_step_raw.astype(jnp.bfloat16), ((0, 0), (0, step_pad)))
    d_unsplit = jnp.concatenate([d_keyval, d_key_vec, d_read_vec], axis=1)
    d_split = jnp.concatenate([d_query, d_mix_in, d_step_wide], axis=1)
    d_projected = jnp.concatenate([d_split, d_mix_gate, d_unsplit], axis=1)
    d_projected, mlp_out = lax.optimization_barrier((d_projected, mlp_out))
    layer_out = (middle + mlp_out.astype(jnp.float32)).astype(jnp.bfloat16)
    d_normed_part = times_trans(d_projected, weights_in)
    first_part = jnp.sum(d_normed_part * hidden * first_scale, axis=0)
    d_normed = lax.psum(d_normed_part.astype(jnp.bfloat16), "tp").astype(jnp.float32)
    in_grads = spread(row_chunks(outer_low(normed, d_split), ctx_size), "ctx")
    unsplit_grads = spread(
        row_chunks(outer_low(normed, d_unsplit), ctx_size * tp_size), ("ctx", "tp")
    )

    per_head = jnp.stack([grad_bias, grad_rate, grad_skip])
    slots = jnp.where(
        (jnp.arange(tp_size, dtype=jnp.int32) == tp_index)[:, None, None], per_head[None], 0.0
    )
    small = lax.psum(
        jnp.concatenate(
            [first_part, jnp.where(tp_index == 0, grad_second, 0.0), slots.reshape(-1)]
        ),
        ("ctx", "tp"),
    )
    head_sums = lax.dynamic_index_in_dim(
        small[2 * width :].reshape(tp_size, 3, heads_local), tp_index, 0, keepdims=False
    )

    grad_hidden = d_middle + norm_back(d_normed, first_gain, hidden, first_scale)

    def summed(received):
        return jnp.sum(received.astype(jnp.float32), axis=0)

    ff_sum = summed(ff_grads)
    out_sum = summed(out_grads)
    in_sum = summed(in_grads)
    unsplit = unsplit_grads.astype(jnp.float32).reshape(
        (ctx_size, tp_size) + unsplit_grads.shape[1:]
    )
    unsplit = jnp.sum(unsplit, axis=0)
    by_head = unsplit[..., : 2 * HEAD]
    by_head = jnp.sum(
        by_head.reshape((KVHEADS, tp_size // KVHEADS) + by_head.shape[1:]), axis=1
    )
    grad_keyval = jnp.concatenate([by_head[head] for head in range(KVHEADS)], axis=-1)
    state_vecs = jnp.sum(unsplit[..., 2 * HEAD :], axis=0)
    q_cols = q_local * HEAD
    return (
        layer_out.reshape(seq_count, row_count, width),
        grad_hidden.reshape(seq_count, row_count, width),
        small[:width],
        in_sum[:, :q_cols],
        grad_keyval,
        out_sum[:, :q_cols].T,
        in_sum[:, q_cols : q_cols + inner_local],
        out_sum[:, q_cols + inner_local :],
        state_vecs[:, :n_state],
        state_vecs[:, n_state:],
        in_sum[:, q_cols + inner_local : q_cols + inner_local + heads_local],
        head_sums[0],
        head_sums[1],
        head_sums[2],
        out_sum[:, q_cols : q_cols + inner_local].T,
        small[width : 2 * width],
        ff_sum[:, :ff_local],
        ff_sum[:, ff_local : 2 * ff_local],
        ff_sum[:, 2 * ff_local :].T,
    )


def solution(mesh):
    placed = (
        P(None, "ctx", None),
        P(),
        P(),
        P(None, "tp"),
        P(),
        P("tp", None),
        P(None, "tp"),
        P(None, "tp"),
        P(),
        P(),
        P(None, "tp"),
        P("tp"),
        P("tp"),
        P("tp"),
        P("tp", None),
        P(),
        P(None, "tp"),
        P(None, "tp"),
        P("tp", None),
        P(None, "ctx", None),
    )
    return jax.shard_map(
        body,
        mesh=mesh,
        in_specs=placed,
        out_specs=(
            P(None, "ctx", None),
            P(None, "ctx", None),
            P(),
            P("ctx", "tp"),
            P(("ctx", "tp"), None),
            P("tp", "ctx"),
            P("ctx", "tp"),
            P("ctx", "tp"),
            P(("ctx", "tp"), None),
            P(("ctx", "tp"), None),
            P("ctx", "tp"),
            P("tp"),
            P("tp"),
            P("tp"),
            P("tp", "ctx"),
            P(),
            P("ctx", "tp"),
            P("ctx", "tp"),
            P("tp", "ctx"),
        ),
        check_vma=False,
    )
```

```python
import jax
import jax.numpy as jnp
from jax import lax
from jax.sharding import PartitionSpec as P

QHEADS = 8
KVHEADS = 2
HEAD = 128


NORM_EPS = 1e-05
MASK_FILL = -1e30
FAR_BELOW = -10000.0
exact_precision = lax.Precision.HIGHEST


def spread(array, axes):
    return lax.all_to_all(array, axes, 0, 0, tiled=True)


def row_chunks(array, count):
    return array.reshape((count, array.shape[0] // count) + array.shape[1:])


def tp_sum(part):
    size = lax.axis_size("tp")
    total = part
    step = 1
    while step < size:
        low_total = total.astype(jnp.bfloat16)
        other = lax.ppermute(low_total, "tp", [(i, i ^ step) for i in range(size)])
        total = low_total.astype(jnp.float32) + other.astype(jnp.float32)
        step *= 2
    return total


def three_parts(value):
    high = lax.reduce_precision(value, 8, 7)
    rest = value - high
    mid = lax.reduce_precision(rest, 8, 7)
    return jnp.stack([high, mid, rest - mid]).astype(jnp.bfloat16)


def decays(step_raw, decay_rate):
    step_size = jax.nn.softplus(step_raw)
    return (step_size, jnp.cumsum(-decay_rate[None, :] * step_size, axis=0))


def state_part(mix_in, key_vec, step_size, log_decay, seg_here, seg_before):
    log_end = log_decay[-1]
    same_end = (seg_here == seg_here[-1]).astype(jnp.float32)
    end_weight = jnp.exp(log_end[None, :] - log_decay) * same_end[:, None] * step_size
    state = jnp.einsum("sh,shp,sn->hpn", end_weight, mix_in, key_vec, precision=exact_precision)
    carried = jnp.exp(log_end) * (seg_here[-1] == seg_before).astype(jnp.float32)
    return (carried, state)


def out_part(
    mix_in, key_vec, read_vec, step_size, log_decay, skip_gain, seg_here, seg_before, state_in
):
    places = jnp.arange(seg_here.shape[0], dtype=jnp.int32)
    visible = (places[:, None] >= places[None, :]) & (seg_here[:, None] == seg_here[None, :])
    log_gap = log_decay[:, None, :] - log_decay[None, :, :]
    weights = jnp.exp(jnp.where(visible[:, :, None], log_gap, FAR_BELOW)) * step_size[None, :, :]
    mixing = jnp.einsum("tn,sn->ts", read_vec, key_vec, precision=exact_precision)
    result = jnp.einsum(
        "tsh,shp->thp", weights * mixing[:, :, None], mix_in, precision=exact_precision
    )
    entry = jnp.exp(log_decay) * (seg_here == seg_before).astype(jnp.float32)[:, None]
    result = result + entry[:, :, None] * jnp.einsum(
        "tn,hpn->thp", read_vec, state_in, precision=exact_precision
    )
    return result + skip_gain[None, :, None] * mix_in


def block_scan(
    mix_in, key_vec, read_vec, step_raw, decay_rate, skip_gain, seg_here, seg_before, state_in
):
    step_size, log_decay = decays(step_raw, decay_rate)
    carried, state = state_part(mix_in, key_vec, step_size, log_decay, seg_here, seg_before)
    result = out_part(
        mix_in, key_vec, read_vec, step_size, log_decay, skip_gain, seg_here, seg_before, state_in
    )
    return (result, carried, state)


def over_blocks(function, axes):
    return jax.vmap(jax.vmap(function, in_axes=axes), in_axes=axes)


def rms_scale(value_rows):
    return lax.rsqrt(jnp.mean(value_rows * value_rows, axis=-1, keepdims=True) + NORM_EPS)


def norm_back(d_norm, gain, value_rows, scale):
    d_hat = d_norm * gain
    return scale * d_hat - value_rows * scale**3 * jnp.mean(
        d_hat * value_rows, axis=-1, keepdims=True
    )


def times_trans(grad, weight_matrix):
    return lax.dot_general(
        grad,
        weight_matrix,
        (((grad.ndim - 1,), (1,)), ((), ())),
        preferred_element_type=jnp.float32,
    )


def outer_rows(left, right):
    return lax.dot_general(
        left, right, (((0,), (0,)), ((), ())), preferred_element_type=jnp.float32
    )


def body(
    hidden_in,
    seg_ids,
    first_gain,
    query_weight,
    keyval_weight,
    attn_out_weight,
    mixin_weight,
    mixgate_weight,
    inject_weight,
    readout_weight,
    step_weight,
    step_bias,
    decay_rate,
    skip_gain,
    mixout_weight,
    second_gain,
    gate_weight,
    up_weight,
    down_weight,
    cotangent,
):
    ctx_size = lax.axis_size("ctx")
    tp_size = lax.axis_size("tp")
    ctx_index = lax.axis_index("ctx")
    tp_index = lax.axis_index("tp")
    seq_count, row_count, width = hidden_in.shape
    block_rows = row_count // 2
    block_count = 2 * ctx_size
    q_local = query_weight.shape[1] // HEAD
    heads_local = step_weight.shape[1]
    inner_local = mixin_weight.shape[1]
    mamba_head = inner_local // heads_local
    n_state = inject_weight.shape[1]
    ff_local = gate_weight.shape[1]
    kv_head = tp_index * q_local // (QHEADS // KVHEADS)
    scale = HEAD ** (-0.5)
    all_rows = seq_count * row_count

    local_rows = jnp.arange(row_count, dtype=jnp.int32)
    devices = jnp.arange(ctx_size, dtype=jnp.int32)

    def positions(device, local):
        return jnp.where(
            local < block_rows,
            device * block_rows + local,
            (block_count - 1 - device) * block_rows + local - block_rows,
        )

    q_places = positions(ctx_index, local_rows)
    k_places = positions(devices[:, None], local_rows[None, :]).reshape(-1)
    seg_by_block = seg_ids.reshape(seq_count, block_count, block_rows)
    k_segs = jnp.concatenate(
        [seg_by_block[:, :ctx_size], seg_by_block[:, ctx_size:][:, ::-1]], axis=2
    ).reshape(seq_count, ctx_size * row_count)
    q_segs = lax.dynamic_slice_in_dim(k_segs, ctx_index * row_count, row_count, 1)
    seg_end = seg_by_block[:, :, -1]
    own_blocks = jnp.stack([ctx_index, block_count - 1 - ctx_index])
    block_ids = jnp.arange(block_count, dtype=jnp.int32)
    is_before = block_ids[None, :] == own_blocks[:, None] - 1
    seg_before = jnp.sum(
        jnp.where(is_before[None], seg_end[:, None, :], 0), axis=-1
    ) - jnp.where(own_blocks == 0, 1, 0)

    step_pad = -heads_local % 128
    step_cols = heads_local + step_pad
    keyval_mine = lax.dynamic_slice_in_dim(keyval_weight, kv_head * 2 * HEAD, 2 * HEAD, 1)
    step_wide = jnp.pad(step_weight, ((0, 0), (0, step_pad)))
    weights_in = jnp.concatenate(
        [
            query_weight,
            mixin_weight,
            step_wide,
            mixgate_weight,
            keyval_mine,
            inject_weight,
            readout_weight,
        ],
        axis=1,
    )
    sizes_in = (
        q_local * HEAD,
        inner_local,
        step_cols,
        inner_local,
        2 * HEAD,
        n_state,
        n_state,
    )
    bounds = []
    at = 0
    for size in sizes_in:
        at += size
        bounds.append(at)

    hidden = hidden_in.astype(jnp.float32).reshape(all_rows, width)
    cotan = cotangent.reshape(all_rows, width)
    first_scale = rms_scale(hidden)
    normed = (hidden * first_scale * first_gain).astype(jnp.bfloat16)
    projected = jnp.dot(normed, weights_in, preferred_element_type=jnp.float32)
    queries, mix_in, step_raw, mix_gate, keyval, key_vec, read_vec = jnp.split(
        projected, bounds[:-1], axis=1
    )
    queries = queries.astype(jnp.bfloat16).reshape(seq_count, row_count, q_local, HEAD)
    keyval = keyval.astype(jnp.bfloat16).reshape(seq_count, row_count, 2 * HEAD)
    mix_in = mix_in.astype(jnp.bfloat16)
    key_vec = key_vec.astype(jnp.bfloat16)
    read_vec = read_vec.astype(jnp.bfloat16)
    step_raw = step_raw[:, :heads_local] + step_bias

    def blocked(value_rows, tail):
        return value_rows.reshape((seq_count, 2, block_rows) + tail)

    mix_blocks = blocked(mix_in.astype(jnp.float32), (heads_local, mamba_head))
    key_blocks = blocked(key_vec.astype(jnp.float32), (n_state,))
    read_blocks = blocked(read_vec.astype(jnp.float32), (n_state,))
    step_blocks = blocked(step_raw, (heads_local,))
    seg_blocks = blocked(q_segs, ())
    step_size, log_decay = over_blocks(decays, (0, None))(step_blocks, decay_rate)

    log_end = (-decay_rate * jnp.sum(step_size, axis=2)).reshape(seq_count, 2 * heads_local)
    parts = jnp.moveaxis(three_parts(log_end), 0, 1).reshape(seq_count, 1, 6 * heads_local)
    extra_rows = jnp.pad(parts, ((0, 0), (0, 15), (0, 2 * HEAD - 6 * heads_local)))
    outgoing = jnp.concatenate([keyval, extra_rows], axis=1)
    gathered = spread(jnp.broadcast_to(outgoing[None], (ctx_size,) + outgoing.shape), "ctx")
    keyval_all = jnp.swapaxes(gathered[:, :, :row_count], 0, 1).reshape(
        seq_count, ctx_size * row_count, 2 * HEAD
    )
    keys_all, values_all = keyval_all[..., :HEAD], keyval_all[..., HEAD:]
    decay_all = jnp.sum(
        gathered[:, :, row_count, : 6 * heads_local]
        .astype(jnp.float32)
        .reshape(ctx_size, seq_count, 3, 2, heads_local),
        axis=2,
    )
    log_blocks = jnp.concatenate([decay_all[:, :, 0], decay_all[::-1, :, 1]], axis=0)
    log_sum = jnp.cumsum(log_blocks, axis=0)

    log_prev = jnp.concatenate([jnp.zeros_like(log_sum[:1]), log_sum[:-1]], axis=0)
    seg_end_t = seg_end.T
    seg_prev_t = jnp.concatenate([jnp.full_like(seg_end_t[:1], -1), seg_end_t[:-1]], axis=0)

    def picked(table):
        return jnp.stack(
            [
                lax.dynamic_index_in_dim(table, own_blocks[0], 0, keepdims=False),
                lax.dynamic_index_in_dim(table, own_blocks[1], 0, keepdims=False),
            ]
        )

    def block_weights(valid, gap):
        weight = jnp.exp(jnp.where(valid[..., None], gap, FAR_BELOW))
        weight = jnp.where(valid[..., None], weight, 0.0)
        halves = jnp.stack([weight[:, :ctx_size], weight[:, ctx_size:][:, ::-1]], axis=2)
        return halves

    order = block_ids[None, :, None]
    own = own_blocks[:, None, None]
    rise = block_weights(
        (order < own) & (seg_end_t[None] == picked(seg_prev_t)[:, None]),
        picked(log_prev)[:, None] - log_sum[None],
    )
    fall = block_weights(
        (order > own) & (seg_prev_t[None] == picked(seg_end_t)[:, None]),
        log_prev[None] - picked(log_sum)[:, None],
    )

    def weighted(weight, blocks):
        total = 0.0
        for half in range(2):
            total = total + jnp.sum(
                weight[:, :, half][..., None, None]
                * blocks[None, :, :, half].astype(jnp.float32),
                axis=1,
            )
        return jnp.swapaxes(total, 0, 1)

    carried, state = over_blocks(state_part, (0, 0, 0, 0, 0, 0))(
        mix_blocks, key_blocks, step_size, log_decay, seg_blocks, seg_before
    )
    state_all = lax.all_gather(state.astype(jnp.bfloat16), "ctx")

    scores = (
        jnp.einsum("srhd,skd->srhk", queries, keys_all, preferred_element_type=jnp.float32) * scale
    )
    visible = (k_places[None, None, :] <= q_places[None, :, None]) & (
        k_segs[:, None, :] == q_segs[:, :, None]
    )
    scores = jnp.where(visible[:, :, None, :], scores, MASK_FILL)
    top = jnp.max(scores, axis=-1, keepdims=True)
    raised = jnp.exp(scores - top)
    probs = raised / jnp.sum(raised, axis=-1, keepdims=True)
    probs_low = probs.astype(jnp.bfloat16)
    attn_full = jnp.einsum(
        "srhk,skd->srhd", probs_low, values_all, preferred_element_type=jnp.float32
    )
    attn_low = attn_full.astype(jnp.bfloat16).reshape(all_rows, q_local * HEAD)

    state_in = weighted(rise, state_all)
    mixed = over_blocks(out_part, (0, 0, 0, 0, 0, None, 0, 0, 0))(
        mix_blocks,
        key_blocks,
        read_blocks,
        step_size,
        log_decay,
        skip_gain,
        seg_blocks,
        seg_before,
        state_in,
    )
    mixed = mixed.reshape(all_rows, inner_local)
    mixgate_sig = jax.nn.sigmoid(mix_gate)
    gate_act = mix_gate * mixgate_sig
    gated = (mixed * gate_act).astype(jnp.bfloat16)
    branch_in = jnp.concatenate([attn_low, gated], axis=1)
    weights_out = jnp.concatenate([attn_out_weight, mixout_weight], axis=0)
    branch = tp_sum(
        jnp.dot(branch_in, weights_out, preferred_element_type=jnp.float32).astype(jnp.bfloat16)
    )
    middle = hidden + branch
    second_scale = rms_scale(middle)
    normed_two = (middle * second_scale * second_gain).astype(jnp.bfloat16)
    weights_ff = jnp.concatenate([gate_weight, up_weight], axis=1)
    gate_up = jnp.dot(normed_two, weights_ff, preferred_element_type=jnp.float32)
    gate, up_val = gate_up[:, :ff_local], gate_up[:, ff_local:]
    gate_sig = jax.nn.sigmoid(gate)
    inner = (gate * gate_sig * up_val).astype(jnp.bfloat16)
    inner_gradient = times_trans(cotan, down_weight)
    d_gate = (inner_gradient * up_val * gate_sig * (1.0 + gate * (1.0 - gate_sig))).astype(
        jnp.bfloat16
    )
    d_up = (inner_gradient * gate * gate_sig).astype(jnp.bfloat16)
    d_gate_up = jnp.concatenate([d_gate, d_up], axis=1)
    second_normed_gradient = tp_sum(times_trans(d_gate_up, weights_ff).astype(jnp.bfloat16))
    mlp_out = lax.psum(
        jnp.dot(inner, down_weight, preferred_element_type=jnp.float32).astype(jnp.bfloat16), "tp"
    )

    def outer_low(left, right):
        return outer_rows(left, right).astype(jnp.bfloat16)

    ff_grads = spread(
        row_chunks(
            jnp.concatenate([outer_low(normed_two, d_gate_up), outer_low(cotan, inner)], axis=1),
            ctx_size,
        ),
        "ctx",
    )

    grad_second = jnp.sum(second_normed_gradient * middle * second_scale, axis=0)
    d_middle = cotan.astype(jnp.float32) + norm_back(
        second_normed_gradient, second_gain, middle, second_scale
    )
    d_branch = d_middle.astype(jnp.bfloat16)
    d_branch_in = times_trans(d_branch, weights_out).astype(jnp.bfloat16)
    d_attn = d_branch_in[:, : q_local * HEAD].reshape(seq_count, row_count, q_local, HEAD)
    d_gated = d_branch_in[:, q_local * HEAD :].astype(jnp.float32)
    d_mixed = d_gated * gate_act
    d_mix_gate = (d_gated * mixed * mixgate_sig * (1.0 + mix_gate * (1.0 - mixgate_sig))).astype(
        jnp.bfloat16
    )

    d_mixed_blocks = blocked(d_mixed, (heads_local, mamba_head))
    entry = (
        jnp.exp(log_decay) * (seg_blocks == seg_before[..., None]).astype(jnp.float32)[..., None]
    )
    local_grad = jnp.einsum(
        "abth,abthp,abtn->abhpn", entry, d_mixed_blocks, read_blocks, precision=exact_precision
    )
    grad_all = lax.all_gather(local_grad.astype(jnp.bfloat16), "ctx")

    delta = jnp.sum(d_attn.astype(jnp.float32) * attn_full, axis=-1, keepdims=True)
    d_probs = jnp.einsum("srhd,skd->srhk", d_attn, values_all, preferred_element_type=jnp.float32)
    d_scores = (probs * (d_probs - delta)).astype(jnp.bfloat16)
    d_keys = (
        jnp.einsum("srhk,srhd->skd", d_scores, queries, preferred_element_type=jnp.float32) * scale
    ).astype(jnp.bfloat16)
    d_values = jnp.einsum(
        "srhk,srhd->skd", probs_low, d_attn, preferred_element_type=jnp.float32
    ).astype(jnp.bfloat16)
    d_keyval = jnp.concatenate([d_keys, d_values], axis=-1).reshape(
        seq_count, ctx_size, row_count, 2 * HEAD
    )
    d_query = (
        jnp.einsum("srhk,skd->srhd", d_scores, keys_all, preferred_element_type=jnp.float32) * scale
    )
    d_query = d_query.astype(jnp.bfloat16).reshape(all_rows, q_local * HEAD)
    mid_grads = row_chunks(
        jnp.concatenate(
            [
                outer_low(d_branch, branch_in),
                outer_low(normed, jnp.concatenate([d_mix_gate, d_query], axis=1)),
            ],
            axis=1,
        ),
        ctx_size,
    )
    keyval_send = jnp.concatenate([d_keyval[seq] for seq in range(seq_count)], axis=-1)
    if mid_grads.shape[1] == row_count:
        received = spread(jnp.concatenate([mid_grads, keyval_send], axis=2), "ctx")
        out_grads = received[..., : mid_grads.shape[2]]
        d_keyval = received[..., mid_grads.shape[2] :]
    else:
        out_grads = spread(mid_grads, "ctx")
        d_keyval = spread(keyval_send, "ctx")
    d_keyval = jnp.sum(d_keyval.astype(jnp.float32), axis=0).astype(jnp.bfloat16)
    d_keyval = jnp.concatenate(jnp.split(d_keyval, seq_count, axis=1), axis=0)

    grad_end = weighted(fall, grad_all)
    decay_cot = jnp.sum(grad_end * state_in, axis=(-2, -1))

    def whole(mix_vals, key_vals, read_vals, step_vals, rate_vals, skip_vals, state_vals):
        return over_blocks(block_scan, (0, 0, 0, 0, None, None, 0, 0, 0))(
            mix_vals,
            key_vals,
            read_vals,
            step_vals,
            rate_vals,
            skip_vals,
            seg_blocks,
            seg_before,
            state_vals,
        )

    _, backward_function = jax.vjp(
        whole, mix_blocks, key_blocks, read_blocks, step_blocks, decay_rate, skip_gain, state_in
    )
    grad_mix, grad_key, grad_read, grad_stepv, grad_rate, grad_skip, _ = backward_function(
        (d_mixed_blocks, decay_cot, grad_end)
    )
    d_mix_in = grad_mix.reshape(all_rows, inner_local).astype(jnp.bfloat16)
    d_key_vec = grad_key.reshape(all_rows, n_state).astype(jnp.bfloat16)
    d_read_vec = grad_read.reshape(all_rows, n_state).astype(jnp.bfloat16)
    d_step_raw = grad_stepv.reshape(all_rows, heads_local)
    grad_bias = jnp.sum(d_step_raw, axis=0)
    d_step_wide = jnp.pad(d_step_raw.astype(jnp.bfloat16), ((0, 0), (0, step_pad)))
    d_unsplit = jnp.concatenate([d_keyval, d_key_vec, d_read_vec], axis=1)
    d_split = jnp.concatenate([d_mix_in, d_step_wide], axis=1)
    d_projected = jnp.concatenate([d_query, d_split, d_mix_gate, d_unsplit], axis=1)
    d_projected, mlp_out = lax.optimization_barrier((d_projected, mlp_out))
    layer_out = (middle + mlp_out.astype(jnp.float32)).astype(jnp.bfloat16)
    d_normed_part = times_trans(d_projected, weights_in)
    first_part = jnp.sum(d_normed_part * hidden * first_scale, axis=0)
    d_normed = tp_sum(d_normed_part.astype(jnp.bfloat16))
    in_grads = spread(row_chunks(outer_low(normed, d_split), ctx_size), "ctx")
    per_head = jnp.stack([grad_bias, grad_rate, grad_skip])
    slots = jnp.where(
        (jnp.arange(tp_size, dtype=jnp.int32) == tp_index)[:, None, None], per_head[None], 0.0
    )
    small = jnp.concatenate(
        [first_part, jnp.where(tp_index == 0, grad_second, 0.0), slots.reshape(-1)]
    )
    small_size = small.shape[0]
    unsplit_cols = d_unsplit.shape[1]
    device_count = ctx_size * tp_size
    small_flat = three_parts(small).reshape(-1)
    small_flat = jnp.pad(small_flat, (0, -small_flat.shape[0] % unsplit_cols))
    small_rows = small_flat.reshape(-1, unsplit_cols)
    unsplit_send = row_chunks(outer_low(normed, d_unsplit), device_count)
    unsplit_rows = unsplit_send.shape[1]
    unsplit_grads = spread(
        jnp.concatenate(
            [
                unsplit_send,
                jnp.broadcast_to(small_rows[None], (device_count,) + small_rows.shape),
            ],
            axis=1,
        ),
        ("ctx", "tp"),
    )
    small = jnp.sum(unsplit_grads[:, unsplit_rows:].astype(jnp.float32), axis=0).reshape(-1)
    small = jnp.sum(small[: 3 * small_size].reshape(3, small_size), axis=0)
    unsplit_grads = unsplit_grads[:, :unsplit_rows]
    head_sums = lax.dynamic_index_in_dim(
        small[2 * width :].reshape(tp_size, 3, heads_local), tp_index, 0, keepdims=False
    )

    grad_hidden = d_middle + norm_back(d_normed, first_gain, hidden, first_scale)

    def summed(received):
        return jnp.sum(received.astype(jnp.float32), axis=0)

    ff_sum = summed(ff_grads)
    out_sum = summed(out_grads)
    in_sum = summed(in_grads)
    unsplit = unsplit_grads.astype(jnp.float32).reshape(
        (ctx_size, tp_size) + unsplit_grads.shape[1:]
    )
    unsplit = jnp.sum(unsplit, axis=0)
    by_head = unsplit[..., : 2 * HEAD]
    by_head = jnp.sum(
        by_head.reshape((KVHEADS, tp_size // KVHEADS) + by_head.shape[1:]), axis=1
    )
    grad_keyval = jnp.concatenate([by_head[head] for head in range(KVHEADS)], axis=-1)
    state_vecs = jnp.sum(unsplit[..., 2 * HEAD :], axis=0)
    q_cols = q_local * HEAD
    return (
        layer_out.reshape(seq_count, row_count, width),
        grad_hidden.reshape(seq_count, row_count, width),
        small[:width],
        out_sum[:, q_cols + 2 * inner_local :],
        grad_keyval,
        out_sum[:, :q_cols].T,
        in_sum[:, :inner_local],
        out_sum[:, q_cols + inner_local : q_cols + 2 * inner_local],
        state_vecs[:, :n_state],
        state_vecs[:, n_state:],
        in_sum[:, inner_local : inner_local + heads_local],
        head_sums[0],
        head_sums[1],
        head_sums[2],
        out_sum[:, q_cols : q_cols + inner_local].T,
        small[width : 2 * width],
        ff_sum[:, :ff_local],
        ff_sum[:, ff_local : 2 * ff_local],
        ff_sum[:, 2 * ff_local :].T,
    )


def solution(mesh):
    placed = (
        P(None, "ctx", None),
        P(),
        P(),
        P(None, "tp"),
        P(),
        P("tp", None),
        P(None, "tp"),
        P(None, "tp"),
        P(),
        P(),
        P(None, "tp"),
        P("tp"),
        P("tp"),
        P("tp"),
        P("tp", None),
        P(),
        P(None, "tp"),
        P(None, "tp"),
        P("tp", None),
        P(None, "ctx", None),
    )
    return jax.shard_map(
        body,
        mesh=mesh,
        in_specs=placed,
        out_specs=(
            P(None, "ctx", None),
            P(None, "ctx", None),
            P(),
            P("ctx", "tp"),
            P(("ctx", "tp"), None),
            P("tp", "ctx"),
            P("ctx", "tp"),
            P("ctx", "tp"),
            P(("ctx", "tp"), None),
            P(("ctx", "tp"), None),
            P("ctx", "tp"),
            P("tp"),
            P("tp"),
            P("tp"),
            P("tp", "ctx"),
            P(),
            P("ctx", "tp"),
            P("ctx", "tp"),
            P("tp", "ctx"),
        ),
        check_vma=False,
    )
```

```python
import jax
import jax.numpy as jnp
from jax import lax
from jax.sharding import PartitionSpec as P

QHEADS = 8
KVHEADS = 2
HEAD = 128


NORM_EPS = 1e-05
MASK_FILL = -1e30
FAR_BELOW = -10000.0
exact_precision = lax.Precision.HIGHEST


def spread(array, axes):
    return lax.all_to_all(array, axes, 0, 0, tiled=True)


def row_chunks(array, count):
    return array.reshape((count, array.shape[0] // count) + array.shape[1:])


def tp_sum(part):
    size = lax.axis_size("tp")
    total = part
    step = 1
    while step < size:
        low_total = total.astype(jnp.bfloat16)
        other = lax.ppermute(low_total, "tp", [(i, i ^ step) for i in range(size)])
        total = low_total.astype(jnp.float32) + other.astype(jnp.float32)
        step *= 2
    return total


def flip(array, step):
    return lax.ppermute(array, "ctx", [(i, i ^ step) for i in range(lax.axis_size("ctx"))])


def ctx_halve(chunks, step):
    bit = (lax.axis_index("ctx") // step) % 2
    pairs = chunks.reshape((chunks.shape[0] // 2, 2) + chunks.shape[1:]).astype(jnp.bfloat16)
    kept = lax.dynamic_index_in_dim(pairs, bit, 1, keepdims=False)
    sent = lax.dynamic_index_in_dim(pairs, 1 - bit, 1, keepdims=False)
    return kept.astype(jnp.float32) + flip(sent, step).astype(jnp.float32)


def ctx_sum(chunks, step=1):
    while chunks.shape[0] > 1:
        chunks = ctx_halve(chunks, step)
        step *= 2
    return chunks[0]


def ctx_all(array):
    index = lax.axis_index("ctx")
    held = array[None]
    step = 1
    while step < lax.axis_size("ctx"):
        upper = (index // step) % 2 == 1
        other = flip(held, step)
        held = jnp.concatenate(
            [jnp.where(upper, other, held), jnp.where(upper, held, other)], axis=0
        )
        step *= 2
    return held


def three_parts(value):
    high = lax.reduce_precision(value, 8, 7)
    rest = value - high
    mid = lax.reduce_precision(rest, 8, 7)
    return jnp.stack([high, mid, rest - mid]).astype(jnp.bfloat16)


def decays(step_raw, decay_rate):
    step_size = jax.nn.softplus(step_raw)
    return (step_size, jnp.cumsum(-decay_rate[None, :] * step_size, axis=0))


def state_part(mix_in, key_vec, step_size, log_decay, seg_here, seg_before):
    log_end = log_decay[-1]
    same_end = (seg_here == seg_here[-1]).astype(jnp.float32)
    end_weight = jnp.exp(log_end[None, :] - log_decay) * same_end[:, None] * step_size
    state = jnp.einsum("sh,shp,sn->hpn", end_weight, mix_in, key_vec, precision=exact_precision)
    carried = jnp.exp(log_end) * (seg_here[-1] == seg_before).astype(jnp.float32)
    return (carried, state)


def out_part(
    mix_in, key_vec, read_vec, step_size, log_decay, skip_gain, seg_here, seg_before, state_in
):
    places = jnp.arange(seg_here.shape[0], dtype=jnp.int32)
    visible = (places[:, None] >= places[None, :]) & (seg_here[:, None] == seg_here[None, :])
    log_gap = log_decay[:, None, :] - log_decay[None, :, :]
    weights = jnp.exp(jnp.where(visible[:, :, None], log_gap, FAR_BELOW)) * step_size[None, :, :]
    mixing = jnp.einsum("tn,sn->ts", read_vec, key_vec, precision=exact_precision)
    result = jnp.einsum(
        "tsh,shp->thp", weights * mixing[:, :, None], mix_in, precision=exact_precision
    )
    entry = jnp.exp(log_decay) * (seg_here == seg_before).astype(jnp.float32)[:, None]
    result = result + entry[:, :, None] * jnp.einsum(
        "tn,hpn->thp", read_vec, state_in, precision=exact_precision
    )
    return result + skip_gain[None, :, None] * mix_in


def block_scan(
    mix_in, key_vec, read_vec, step_raw, decay_rate, skip_gain, seg_here, seg_before, state_in
):
    step_size, log_decay = decays(step_raw, decay_rate)
    carried, state = state_part(mix_in, key_vec, step_size, log_decay, seg_here, seg_before)
    result = out_part(
        mix_in, key_vec, read_vec, step_size, log_decay, skip_gain, seg_here, seg_before, state_in
    )
    return (result, carried, state)


def over_blocks(function, axes):
    return jax.vmap(jax.vmap(function, in_axes=axes), in_axes=axes)


def rms_scale(value_rows):
    return lax.rsqrt(jnp.mean(value_rows * value_rows, axis=-1, keepdims=True) + NORM_EPS)


def norm_back(d_norm, gain, value_rows, scale):
    d_hat = d_norm * gain
    return scale * d_hat - value_rows * scale**3 * jnp.mean(
        d_hat * value_rows, axis=-1, keepdims=True
    )


def times_trans(grad, weight_matrix):
    return lax.dot_general(
        grad,
        weight_matrix,
        (((grad.ndim - 1,), (1,)), ((), ())),
        preferred_element_type=jnp.float32,
    )


def outer_rows(left, right):
    return lax.dot_general(
        left, right, (((0,), (0,)), ((), ())), preferred_element_type=jnp.float32
    )


def body(
    hidden_in,
    seg_ids,
    first_gain,
    query_weight,
    keyval_weight,
    attn_out_weight,
    mixin_weight,
    mixgate_weight,
    inject_weight,
    readout_weight,
    step_weight,
    step_bias,
    decay_rate,
    skip_gain,
    mixout_weight,
    second_gain,
    gate_weight,
    up_weight,
    down_weight,
    cotangent,
):
    ctx_size = lax.axis_size("ctx")
    tp_size = lax.axis_size("tp")
    ctx_index = lax.axis_index("ctx")
    tp_index = lax.axis_index("tp")
    seq_count, row_count, width = hidden_in.shape
    block_rows = row_count // 2
    block_count = 2 * ctx_size
    q_local = query_weight.shape[1] // HEAD
    heads_local = step_weight.shape[1]
    inner_local = mixin_weight.shape[1]
    mamba_head = inner_local // heads_local
    n_state = inject_weight.shape[1]
    ff_local = gate_weight.shape[1]
    kv_head = tp_index * q_local // (QHEADS // KVHEADS)
    scale = HEAD ** (-0.5)
    all_rows = seq_count * row_count

    local_rows = jnp.arange(row_count, dtype=jnp.int32)
    devices = jnp.arange(ctx_size, dtype=jnp.int32)

    def positions(device, local):
        return jnp.where(
            local < block_rows,
            device * block_rows + local,
            (block_count - 1 - device) * block_rows + local - block_rows,
        )

    q_places = positions(ctx_index, local_rows)
    k_places = positions(devices[:, None], local_rows[None, :]).reshape(-1)
    seg_by_block = seg_ids.reshape(seq_count, block_count, block_rows)
    k_segs = jnp.concatenate(
        [seg_by_block[:, :ctx_size], seg_by_block[:, ctx_size:][:, ::-1]], axis=2
    ).reshape(seq_count, ctx_size * row_count)
    q_segs = lax.dynamic_slice_in_dim(k_segs, ctx_index * row_count, row_count, 1)
    seg_end = seg_by_block[:, :, -1]
    own_blocks = jnp.stack([ctx_index, block_count - 1 - ctx_index])
    block_ids = jnp.arange(block_count, dtype=jnp.int32)
    is_before = block_ids[None, :] == own_blocks[:, None] - 1
    seg_before = jnp.sum(
        jnp.where(is_before[None], seg_end[:, None, :], 0), axis=-1
    ) - jnp.where(own_blocks == 0, 1, 0)

    step_pad = -heads_local % 128
    step_cols = heads_local + step_pad
    keyval_mine = lax.dynamic_slice_in_dim(keyval_weight, kv_head * 2 * HEAD, 2 * HEAD, 1)
    step_wide = jnp.pad(step_weight, ((0, 0), (0, step_pad)))
    weights_in = jnp.concatenate(
        [
            query_weight,
            mixin_weight,
            step_wide,
            mixgate_weight,
            keyval_mine,
            inject_weight,
            readout_weight,
        ],
        axis=1,
    )
    sizes_in = (
        q_local * HEAD,
        inner_local,
        step_cols,
        inner_local,
        2 * HEAD,
        n_state,
        n_state,
    )
    bounds = []
    at = 0
    for size in sizes_in:
        at += size
        bounds.append(at)

    hidden = hidden_in.astype(jnp.float32).reshape(all_rows, width)
    cotan = cotangent.reshape(all_rows, width)
    first_scale = rms_scale(hidden)
    normed = (hidden * first_scale * first_gain).astype(jnp.bfloat16)
    projected = jnp.dot(normed, weights_in, preferred_element_type=jnp.float32)
    queries, mix_in, step_raw, mix_gate, keyval, key_vec, read_vec = jnp.split(
        projected, bounds[:-1], axis=1
    )
    queries = queries.astype(jnp.bfloat16).reshape(seq_count, row_count, q_local, HEAD)
    keyval = keyval.astype(jnp.bfloat16).reshape(seq_count, row_count, 2 * HEAD)
    mix_in = mix_in.astype(jnp.bfloat16)
    key_vec = key_vec.astype(jnp.bfloat16)
    read_vec = read_vec.astype(jnp.bfloat16)
    step_raw = step_raw[:, :heads_local] + step_bias

    def blocked(value_rows, tail):
        return value_rows.reshape((seq_count, 2, block_rows) + tail)

    mix_blocks = blocked(mix_in.astype(jnp.float32), (heads_local, mamba_head))
    key_blocks = blocked(key_vec.astype(jnp.float32), (n_state,))
    read_blocks = blocked(read_vec.astype(jnp.float32), (n_state,))
    step_blocks = blocked(step_raw, (heads_local,))
    seg_blocks = blocked(q_segs, ())
    step_size, log_decay = over_blocks(decays, (0, None))(step_blocks, decay_rate)

    log_end = (-decay_rate * jnp.sum(step_size, axis=2)).reshape(seq_count, 2 * heads_local)
    parts = jnp.moveaxis(three_parts(log_end), 0, 1).reshape(seq_count, 1, 6 * heads_local)
    extra_rows = jnp.pad(parts, ((0, 0), (0, 15), (0, 2 * HEAD - 6 * heads_local)))
    outgoing = jnp.concatenate([keyval, extra_rows], axis=1)
    gathered = ctx_all(outgoing)
    keyval_all = jnp.swapaxes(gathered[:, :, :row_count], 0, 1).reshape(
        seq_count, ctx_size * row_count, 2 * HEAD
    )
    keys_all, values_all = keyval_all[..., :HEAD], keyval_all[..., HEAD:]
    decay_all = jnp.sum(
        gathered[:, :, row_count, : 6 * heads_local]
        .astype(jnp.float32)
        .reshape(ctx_size, seq_count, 3, 2, heads_local),
        axis=2,
    )
    log_blocks = jnp.concatenate([decay_all[:, :, 0], decay_all[::-1, :, 1]], axis=0)
    log_sum = jnp.cumsum(log_blocks, axis=0)

    log_prev = jnp.concatenate([jnp.zeros_like(log_sum[:1]), log_sum[:-1]], axis=0)
    seg_end_t = seg_end.T
    seg_prev_t = jnp.concatenate([jnp.full_like(seg_end_t[:1], -1), seg_end_t[:-1]], axis=0)

    def picked(table):
        return jnp.stack(
            [
                lax.dynamic_index_in_dim(table, own_blocks[0], 0, keepdims=False),
                lax.dynamic_index_in_dim(table, own_blocks[1], 0, keepdims=False),
            ]
        )

    def block_weights(valid, gap):
        weight = jnp.exp(jnp.where(valid[..., None], gap, FAR_BELOW))
        weight = jnp.where(valid[..., None], weight, 0.0)
        halves = jnp.stack([weight[:, :ctx_size], weight[:, ctx_size:][:, ::-1]], axis=2)
        return halves

    order = block_ids[None, :, None]
    own = own_blocks[:, None, None]
    rise = block_weights(
        (order < own) & (seg_end_t[None] == picked(seg_prev_t)[:, None]),
        picked(log_prev)[:, None] - log_sum[None],
    )
    fall = block_weights(
        (order > own) & (seg_prev_t[None] == picked(seg_end_t)[:, None]),
        log_prev[None] - picked(log_sum)[:, None],
    )

    def weighted(weight, blocks):
        total = 0.0
        for half in range(2):
            total = total + jnp.sum(
                weight[:, :, half][..., None, None]
                * blocks[None, :, :, half].astype(jnp.float32),
                axis=1,
            )
        return jnp.swapaxes(total, 0, 1)

    carried, state = over_blocks(state_part, (0, 0, 0, 0, 0, 0))(
        mix_blocks, key_blocks, step_size, log_decay, seg_blocks, seg_before
    )
    state_all = lax.all_gather(state.astype(jnp.bfloat16), "ctx")

    scores = (
        jnp.einsum("srhd,skd->srhk", queries, keys_all, preferred_element_type=jnp.float32) * scale
    )
    visible = (k_places[None, None, :] <= q_places[None, :, None]) & (
        k_segs[:, None, :] == q_segs[:, :, None]
    )
    scores = jnp.where(visible[:, :, None, :], scores, MASK_FILL)
    top = jnp.max(scores, axis=-1, keepdims=True)
    raised = jnp.exp(scores - top)
    probs = raised / jnp.sum(raised, axis=-1, keepdims=True)
    probs_low = probs.astype(jnp.bfloat16)
    attn_full = jnp.einsum(
        "srhk,skd->srhd", probs_low, values_all, preferred_element_type=jnp.float32
    )
    attn_low = attn_full.astype(jnp.bfloat16).reshape(all_rows, q_local * HEAD)

    state_in = weighted(rise, state_all)
    mixed = over_blocks(out_part, (0, 0, 0, 0, 0, None, 0, 0, 0))(
        mix_blocks,
        key_blocks,
        read_blocks,
        step_size,
        log_decay,
        skip_gain,
        seg_blocks,
        seg_before,
        state_in,
    )
    mixed = mixed.reshape(all_rows, inner_local)
    mixgate_sig = jax.nn.sigmoid(mix_gate)
    gate_act = mix_gate * mixgate_sig
    gated = (mixed * gate_act).astype(jnp.bfloat16)
    branch_in = jnp.concatenate([attn_low, gated], axis=1)
    weights_out = jnp.concatenate([attn_out_weight, mixout_weight], axis=0)
    branch = tp_sum(
        jnp.dot(branch_in, weights_out, preferred_element_type=jnp.float32).astype(jnp.bfloat16)
    )
    middle = hidden + branch
    second_scale = rms_scale(middle)
    normed_two = (middle * second_scale * second_gain).astype(jnp.bfloat16)
    weights_ff = jnp.concatenate([gate_weight, up_weight], axis=1)
    gate_up = jnp.dot(normed_two, weights_ff, preferred_element_type=jnp.float32)
    gate, up_val = gate_up[:, :ff_local], gate_up[:, ff_local:]
    gate_sig = jax.nn.sigmoid(gate)
    inner = (gate * gate_sig * up_val).astype(jnp.bfloat16)
    inner_gradient = times_trans(cotan, down_weight)
    d_gate = (inner_gradient * up_val * gate_sig * (1.0 + gate * (1.0 - gate_sig))).astype(
        jnp.bfloat16
    )
    d_up = (inner_gradient * gate * gate_sig).astype(jnp.bfloat16)
    d_gate_up = jnp.concatenate([d_gate, d_up], axis=1)
    second_normed_gradient = tp_sum(times_trans(d_gate_up, weights_ff).astype(jnp.bfloat16))
    mlp_out = lax.psum(
        jnp.dot(inner, down_weight, preferred_element_type=jnp.float32).astype(jnp.bfloat16), "tp"
    )

    def outer_low(left, right):
        return outer_rows(left, right).astype(jnp.bfloat16)

    ff_sum = ctx_sum(
        row_chunks(
            jnp.concatenate([outer_low(normed_two, d_gate_up), outer_low(cotan, inner)], axis=1),
            ctx_size,
        )
    )

    grad_second = jnp.sum(second_normed_gradient * middle * second_scale, axis=0)
    d_middle = cotan.astype(jnp.float32) + norm_back(
        second_normed_gradient, second_gain, middle, second_scale
    )
    d_branch = d_middle.astype(jnp.bfloat16)
    d_branch_in = times_trans(d_branch, weights_out).astype(jnp.bfloat16)
    d_attn = d_branch_in[:, : q_local * HEAD].reshape(seq_count, row_count, q_local, HEAD)
    d_gated = d_branch_in[:, q_local * HEAD :].astype(jnp.float32)
    d_mixed = d_gated * gate_act
    d_mix_gate = (d_gated * mixed * mixgate_sig * (1.0 + mix_gate * (1.0 - mixgate_sig))).astype(
        jnp.bfloat16
    )

    d_mixed_blocks = blocked(d_mixed, (heads_local, mamba_head))
    entry = (
        jnp.exp(log_decay) * (seg_blocks == seg_before[..., None]).astype(jnp.float32)[..., None]
    )
    local_grad = jnp.einsum(
        "abth,abthp,abtn->abhpn", entry, d_mixed_blocks, read_blocks, precision=exact_precision
    )
    grad_all = lax.all_gather(local_grad.astype(jnp.bfloat16), "ctx")

    delta = jnp.sum(d_attn.astype(jnp.float32) * attn_full, axis=-1, keepdims=True)
    d_probs = jnp.einsum("srhd,skd->srhk", d_attn, values_all, preferred_element_type=jnp.float32)
    d_scores = (probs * (d_probs - delta)).astype(jnp.bfloat16)
    d_keys = (
        jnp.einsum("srhk,srhd->skd", d_scores, queries, preferred_element_type=jnp.float32) * scale
    ).astype(jnp.bfloat16)
    d_values = jnp.einsum(
        "srhk,srhd->skd", probs_low, d_attn, preferred_element_type=jnp.float32
    ).astype(jnp.bfloat16)
    d_keyval = jnp.concatenate([d_keys, d_values], axis=-1).reshape(
        seq_count, ctx_size, row_count, 2 * HEAD
    )
    d_query = (
        jnp.einsum("srhk,skd->srhd", d_scores, keys_all, preferred_element_type=jnp.float32) * scale
    )
    d_query = d_query.astype(jnp.bfloat16).reshape(all_rows, q_local * HEAD)
    mid_grads = row_chunks(
        jnp.concatenate(
            [
                outer_low(d_branch, branch_in),
                outer_low(normed, jnp.concatenate([d_mix_gate, d_query], axis=1)),
            ],
            axis=1,
        ),
        ctx_size,
    )
    keyval_send = jnp.concatenate([d_keyval[seq] for seq in range(seq_count)], axis=-1)
    grad_all, ff_sum = lax.optimization_barrier((grad_all, ff_sum))
    grad_end = weighted(fall, grad_all)
    decay_cot = jnp.sum(grad_end * state_in, axis=(-2, -1))
    if mid_grads.shape[1] == row_count:
        received = ctx_halve(jnp.concatenate([mid_grads, keyval_send], axis=2), 1)
        decay_cot, received = lax.optimization_barrier((decay_cot, received.astype(jnp.bfloat16)))
        received = ctx_sum(received, 2)
        out_sum = received[:, : mid_grads.shape[2]]
        d_keyval = received[:, mid_grads.shape[2] :]
    else:
        out_sum = ctx_sum(mid_grads)
        d_keyval = ctx_sum(keyval_send)
    d_keyval = d_keyval.astype(jnp.bfloat16)
    d_keyval = jnp.concatenate(jnp.split(d_keyval, seq_count, axis=1), axis=0)

    def whole(mix_vals, key_vals, read_vals, step_vals, rate_vals, skip_vals, state_vals):
        return over_blocks(block_scan, (0, 0, 0, 0, None, None, 0, 0, 0))(
            mix_vals,
            key_vals,
            read_vals,
            step_vals,
            rate_vals,
            skip_vals,
            seg_blocks,
            seg_before,
            state_vals,
        )

    _, backward_function = jax.vjp(
        whole, mix_blocks, key_blocks, read_blocks, step_blocks, decay_rate, skip_gain, state_in
    )
    grad_mix, grad_key, grad_read, grad_stepv, grad_rate, grad_skip, _ = backward_function(
        (d_mixed_blocks, decay_cot, grad_end)
    )
    d_mix_in = grad_mix.reshape(all_rows, inner_local).astype(jnp.bfloat16)
    d_key_vec = grad_key.reshape(all_rows, n_state).astype(jnp.bfloat16)
    d_read_vec = grad_read.reshape(all_rows, n_state).astype(jnp.bfloat16)
    d_step_raw = grad_stepv.reshape(all_rows, heads_local)
    grad_bias = jnp.sum(d_step_raw, axis=0)
    d_step_wide = jnp.pad(d_step_raw.astype(jnp.bfloat16), ((0, 0), (0, step_pad)))
    d_unsplit = jnp.concatenate([d_keyval, d_key_vec, d_read_vec], axis=1)
    d_split = jnp.concatenate([d_mix_in, d_step_wide], axis=1)
    d_projected = jnp.concatenate([d_query, d_split, d_mix_gate, d_unsplit], axis=1)
    d_projected, mlp_out = lax.optimization_barrier((d_projected, mlp_out))
    layer_out = (middle + mlp_out.astype(jnp.float32)).astype(jnp.bfloat16)
    d_normed_part = times_trans(d_projected, weights_in)
    first_part = jnp.sum(d_normed_part * hidden * first_scale, axis=0)
    d_normed = tp_sum(d_normed_part.astype(jnp.bfloat16))
    in_sum = ctx_sum(row_chunks(outer_low(normed, d_split), ctx_size))
    per_head = jnp.stack([grad_bias, grad_rate, grad_skip])
    slots = jnp.where(
        (jnp.arange(tp_size, dtype=jnp.int32) == tp_index)[:, None, None], per_head[None], 0.0
    )
    small = jnp.concatenate(
        [first_part, jnp.where(tp_index == 0, grad_second, 0.0), slots.reshape(-1)]
    )
    small_size = small.shape[0]
    unsplit_cols = d_unsplit.shape[1]
    device_count = ctx_size * tp_size
    small_flat = three_parts(small).reshape(-1)
    small_flat = jnp.pad(small_flat, (0, -small_flat.shape[0] % unsplit_cols))
    small_rows = small_flat.reshape(-1, unsplit_cols)
    unsplit_send = row_chunks(outer_low(normed, d_unsplit), device_count)
    unsplit_rows = unsplit_send.shape[1]
    unsplit_grads = spread(
        jnp.concatenate(
            [
                unsplit_send,
                jnp.broadcast_to(small_rows[None], (device_count,) + small_rows.shape),
            ],
            axis=1,
        ),
        ("ctx", "tp"),
    )
    small = jnp.sum(unsplit_grads[:, unsplit_rows:].astype(jnp.float32), axis=0).reshape(-1)
    small = jnp.sum(small[: 3 * small_size].reshape(3, small_size), axis=0)
    unsplit_grads = unsplit_grads[:, :unsplit_rows]
    head_sums = lax.dynamic_index_in_dim(
        small[2 * width :].reshape(tp_size, 3, heads_local), tp_index, 0, keepdims=False
    )

    grad_hidden = d_middle + norm_back(d_normed, first_gain, hidden, first_scale)

    unsplit = unsplit_grads.astype(jnp.float32).reshape(
        (ctx_size, tp_size) + unsplit_grads.shape[1:]
    )
    unsplit = jnp.sum(unsplit, axis=0)
    by_head = unsplit[..., : 2 * HEAD]
    by_head = jnp.sum(
        by_head.reshape((KVHEADS, tp_size // KVHEADS) + by_head.shape[1:]), axis=1
    )
    grad_keyval = jnp.concatenate([by_head[head] for head in range(KVHEADS)], axis=-1)
    state_vecs = jnp.sum(unsplit[..., 2 * HEAD :], axis=0)
    q_cols = q_local * HEAD
    return (
        layer_out.reshape(seq_count, row_count, width),
        grad_hidden.reshape(seq_count, row_count, width),
        small[:width],
        out_sum[:, q_cols + 2 * inner_local :],
        grad_keyval,
        out_sum[:, :q_cols].T,
        in_sum[:, :inner_local],
        out_sum[:, q_cols + inner_local : q_cols + 2 * inner_local],
        state_vecs[:, :n_state],
        state_vecs[:, n_state:],
        in_sum[:, inner_local : inner_local + heads_local],
        head_sums[0],
        head_sums[1],
        head_sums[2],
        out_sum[:, q_cols : q_cols + inner_local].T,
        small[width : 2 * width],
        ff_sum[:, :ff_local],
        ff_sum[:, ff_local : 2 * ff_local],
        ff_sum[:, 2 * ff_local :].T,
    )


def solution(mesh):
    placed = (
        P(None, "ctx", None),
        P(),
        P(),
        P(None, "tp"),
        P(),
        P("tp", None),
        P(None, "tp"),
        P(None, "tp"),
        P(),
        P(),
        P(None, "tp"),
        P("tp"),
        P("tp"),
        P("tp"),
        P("tp", None),
        P(),
        P(None, "tp"),
        P(None, "tp"),
        P("tp", None),
        P(None, "ctx", None),
    )
    return jax.shard_map(
        body,
        mesh=mesh,
        in_specs=placed,
        out_specs=(
            P(None, "ctx", None),
            P(None, "ctx", None),
            P(),
            P("ctx", "tp"),
            P(("ctx", "tp"), None),
            P("tp", "ctx"),
            P("ctx", "tp"),
            P("ctx", "tp"),
            P(("ctx", "tp"), None),
            P(("ctx", "tp"), None),
            P("ctx", "tp"),
            P("tp"),
            P("tp"),
            P("tp"),
            P("tp", "ctx"),
            P(),
            P("ctx", "tp"),
            P("ctx", "tp"),
            P("tp", "ctx"),
        ),
        check_vma=False,
    )
```
